32 devices in a mesh: section: 2 (over core), dp: 8 (over z, x), fsdp: 2 (over y).
Axes of the slice: x: 2, y: 2, z: 4, core: 2. Of those that a mesh axis runs over, the one named last changes fastest.
Arguments:
- images: bfloat16 [96, 196, 512], P(('dp', 'fsdp')), may hold values from -6 to 6
- out_grad: bfloat16 [96, 196, 512], P(('dp', 'fsdp')), may hold values from -6 to 6
- live: int32 [16, 2], P(('dp', 'fsdp')), may hold values from 0 to 3, as said below
- qkv_w: bfloat16 [2, 512, 1536], P('section', 'fsdp'), may hold values from -0.25 to 0.25
- proj_w: bfloat16 [2, 512, 512], P('section', 'fsdp'), may hold values from -0.75 to 0.75
- fc1_w: bfloat16 [2, 512, 2048], P('section', 'fsdp'), may hold values from -0.25 to 0.25
- fc2_w: bfloat16 [2, 2048, 512], P('section', 'fsdp'), may hold values from -0.125 to 0.125
- gains: bfloat16 [2, 2, 512], P('section', None, 'fsdp'), may hold values from 0.5 to 1.5
- biases: bfloat16 [2, 6, 512], P('section', None, 'fsdp'), may hold values from -1.796875 to 1.796875
- hidden_bias: bfloat16 [2, 2048], P('section', 'fsdp'), may hold values from -1.796875 to 1.796875
- table: float32 [2, 169, 16], P('section'), may hold values from -6 to 6
- rel_index: int32 [49, 49], replicated, may hold values from 0 to 168
- region: int32 [196], replicated, may hold values from 0 to 3
Outputs:
- layer_out: bfloat16 [2, 96, 196, 512], P('section', ('dp', 'fsdp'))
- input_grad: bfloat16 [2, 96, 196, 512], P('section', ('dp', 'fsdp'))
- d_qkv_w: float32 [2, 512, 1536], P('section', 'fsdp')
- d_proj_w: float32 [2, 512, 512], P('section', 'fsdp')
- d_fc1_w: float32 [2, 512, 2048], P('section', 'fsdp')
- d_fc2_w: float32 [2, 2048, 512], P('section', 'fsdp')
- d_gains: float32 [2, 2, 512], P('section', None, 'fsdp')
- d_biases: float32 [2, 6, 512], P('section', None, 'fsdp')
- d_hidden_bias: float32 [2, 2048], P('section', 'fsdp')
- d_table: float32 [2, 169, 16], P('section')
- d_query_bias: float32 [2, 512], P('section', 'fsdp')
The draws below stay inside these ranges and needn't reach their ends.
Inputs may be any that keep to these rules, and one draw needn't show every extreme that they name: The first live[s, m] of the 3 slots of micro-batch m of shard s are live; in every draw some shard has all 3 live in some micro-batch.
All inputs are finite; a program needn't handle non-finite values.
Results may differ from the reference program's by a relative error of at most 0.018.
Values may be sent and summed in bfloat16 or wider, within the bound.
A program may use at most 256 MiB of HBM per device.

```python
import jax
import jax.numpy as jnp
from jax import lax

D = 512
HEADS = 16
FF = 2048
HEAD_DIM = 32
GRID = 14
WIN = 7
TOK = 196
WTOK = 49
NWIN = 4
TABLE = 169
MB = 2
IPM = 3
IMG_DEV = 6
DATA = 16
IMAGES = 96
N_SECTION = 2


def draw_live(key, part):
    key = jax.random.fold_in(key, 3)
    first_key, second_key = jax.random.split(key)
    counts = jax.random.randint(first_key, (DATA * MB,), 0, IPM + 1)
    chosen = jax.random.randint(second_key, (), 0, DATA * MB)
    counts = jnp.where(jnp.arange(DATA * MB) == chosen, IPM, counts)
    return counts.reshape(DATA, MB).astype(jnp.int32)


def plant(result, rng, least, top_value):
    longest = result.shape.index(max(result.shape))
    spots = []
    for shift in (0, 1):
        where = [jax.random.randint(jax.random.fold_in(rng, axis), (), 0, length) for axis, length in enumerate(result.shape)]
        where[longest] = (where[longest] + shift) % result.shape[longest]
        spots.append(tuple(where))
    return result.at[spots[0]].set(least).at[spots[1]].set(top_value)


def block_scale(key, dims, cuts, smallest, high):
    factor_of = 1.0
    for dim, parts in cuts:
        steps = jax.random.uniform(jax.random.fold_in(jax.random.fold_in(key, 6), dim), (parts,), jnp.float32, smallest / len(cuts), high / len(cuts))
        factor_of = factor_of * jnp.repeat(jnp.exp(steps), dims[dim] // parts).reshape((-1,) + (1,) * (len(dims) - 1 - dim))
    return factor_of


def noise(rng, dims, width, bound, cuts=(), held_as=jnp.bfloat16):
    result = jax.random.normal(rng, dims, jnp.float32) * width
    if len(cuts) > 0:
        result = block_scale(rng, dims, cuts, -0.22, 0.18) * result
    return jnp.clip(result, min=-bound, max=bound).astype(held_as)


def setup_inputs(seed: int = 0) -> dict:
    splits = jax.random.split(jax.random.key(seed), 14)
    images = noise(splits[0], (IMAGES, TOK, D), 1.0, 6.0, ((0, 16),))
    out_grad = noise(splits[1], (IMAGES, TOK, D), 1.0, 6.0, ((0, 16),))
    live = draw_live(jax.random.fold_in(splits[13], 71), 0)
    qkv_w = noise(splits[3], (N_SECTION, D, 3 * D), D ** -0.5, 0.25, ((0, 2), (1, 2)))
    proj_w = noise(splits[4], (N_SECTION, D, D), (D // 8) ** -0.5, 0.75, ((0, 2), (1, 2)))
    fc1_w = noise(splits[5], (N_SECTION, D, FF), D ** -0.5, 0.25, ((0, 2), (1, 2)))
    fc2_w = noise(splits[6], (N_SECTION, FF, D), FF ** -0.5, 0.125, ((0, 2), (1, 2)))
    gains = jnp.clip(1.0 + 0.1 * jax.random.normal(splits[7], (N_SECTION, 2, D), jnp.float32), 0.5, 1.5).astype(jnp.bfloat16)
    biases = noise(splits[8], (N_SECTION, 6, D), 0.3, 1.796875, ((0, 2), (2, 2)))
    hidden_bias = noise(splits[9], (N_SECTION, FF), 0.3, 1.796875, ((0, 2), (1, 2)))
    table = noise(splits[10], (N_SECTION, TABLE, HEADS), 1.0, 6.0, ((0, 2),), jnp.float32)
    rel_index = plant(jax.random.randint(splits[11], (WTOK, WTOK), 0, TABLE), jax.random.fold_in(splits[11], 1), 0, TABLE - 1).astype(jnp.int32)
    region = plant(jax.random.randint(splits[12], (TOK,), 0, 4), jax.random.fold_in(splits[12], 1), 0, 3).astype(jnp.int32)
    return dict(images=images, out_grad=out_grad, live=live, qkv_w=qkv_w, proj_w=proj_w, fc1_w=fc1_w, fc2_w=fc2_w, gains=gains, biases=biases, hidden_bias=hidden_bias, table=table, rel_index=rel_index, region=region)


@jax.custom_vjp
def low(v):
    return lax.optimization_barrier(v.astype(jnp.bfloat16)).astype(jnp.float32)

@jax.custom_vjp
def low_back(v):
    return v

def low_keep(v):
    return (low(v), None)

def low_pass(kept, grad):
    return (grad,)

def back_keep(v):
    return (v, None)

def back_low(kept, grad):
    return (low(grad),)
low.defvjp(low_keep, low_pass)
low_back.defvjp(back_keep, back_low)
HIGH = lax.Precision.HIGHEST
EPS = 1e-05

def norm(values, gain, offset):
    middle = lax.optimization_barrier(jnp.mean(values, -1, keepdims=True))
    centred = values - middle
    spread = lax.optimization_barrier(jnp.mean(centred * centred, -1, keepdims=True))
    return centred * lax.rsqrt(spread + EPS) * gain + offset

def to_windows(grid):
    batch, side, _, depth = grid.shape
    across = side // WIN
    tiles = grid.reshape(batch, across, WIN, across, WIN, depth).transpose(0, 1, 3, 2, 4, 5)
    return tiles.reshape(batch, across * across, WIN * WIN, depth)

def from_windows(tiles):
    batch, _, _, depth = tiles.shape
    across = GRID // WIN
    grid = tiles.reshape(batch, across, across, WIN, WIN, depth).transpose(0, 1, 3, 2, 4, 5)
    return grid.reshape(batch, GRID, GRID, depth)

def swin_layer(source, weights, shifted, rel_index, region):
    qkv_w, proj_w, fc1_w, fc2_w, gains, biases, hidden_bias, table = weights
    batch = source.shape[0]
    moved = WIN // 2
    normed = low(norm(source, gains[0], biases[0]))
    grid = normed.reshape(batch, GRID, GRID, D)
    if shifted:
        grid = jnp.roll(grid, (-moved, -moved), (1, 2))
    windows = to_windows(grid)
    qkv_bias = jnp.concatenate([biases[1], jnp.zeros_like(biases[1]), biases[2]])
    packed = jnp.einsum('bwtc,ce->bwte', windows, qkv_w, precision=HIGH) + qkv_bias
    packed = low(low_back(packed))
    head_shape = (batch, NWIN, WTOK, HEADS, HEAD_DIM)
    query = packed[..., :D].reshape(head_shape)
    keys = packed[..., D:2 * D].reshape(head_shape)
    values = packed[..., 2 * D:].reshape(head_shape)
    rel_bias = table[rel_index].transpose(2, 0, 1)
    scores = jnp.einsum('bwqhd,bwkhd->bwhqk', query, keys, precision=HIGH) * HEAD_DIM ** (-0.5)
    scores = scores + rel_bias[None, None]
    if shifted:
        region_win = to_windows(region.reshape(1, GRID, GRID, 1)).reshape(NWIN, WTOK)
        mask_add = jnp.where(region_win[:, :, None] != region_win[:, None, :], -100.0, 0.0).astype(jnp.float32)
        scores = scores + mask_add[None, :, None]
    scores = low_back(scores)
    probs = jax.nn.softmax(scores, axis=-1)
    mixed = jnp.einsum('bwhqk,bwkhd->bwqhd', low(probs), values, precision=HIGH)
    mixed = low(low_back(mixed)).reshape(batch, NWIN, WTOK, D)
    projected = low_back(jnp.einsum('bwtc,ce->bwte', mixed, proj_w, precision=HIGH) + biases[3])
    back = from_windows(projected)
    if shifted:
        back = jnp.roll(back, (moved, moved), (1, 2))
    middle = source + back.reshape(batch, TOK, D)
    normed2 = low(norm(middle, gains[1], biases[4]))
    hidden = low_back(jnp.einsum('btc,cf->btf', normed2, fc1_w, precision=HIGH) + hidden_bias)
    active = low(jax.nn.gelu(hidden, approximate=False))
    return middle + jnp.einsum('btf,fc->btc', active, fc2_w, precision=HIGH) + biases[5]

def reference(images, out_grad, live, qkv_w, proj_w, fc1_w, fc2_w, gains, biases, hidden_bias, table, rel_index, region):
    params = tuple((a.astype(jnp.float32) for a in (qkv_w, proj_w, fc1_w, fc2_w, gains, biases, hidden_bias, table)))
    inputs = images.astype(jnp.float32).reshape(DATA, IMG_DEV, TOK, D)
    cotangent = out_grad.astype(jnp.float32).reshape(DATA, IMG_DEV, TOK, D)
    slots = jnp.arange(IMG_DEV, dtype=jnp.int32) % IPM
    keep = (slots[None, :] < jnp.repeat(live, IPM, axis=1)).astype(jnp.float32)
    zero_pad = jnp.zeros_like(inputs)

    def total(inputs, zero_pad, params):
        first_params = tuple((p[0] for p in params))
        second_params = tuple((p[1] for p in params))

        def block(pieces):
            source, zero_part, cot_part, keep_part = pieces
            first = low(swin_layer(source, first_params, False, rel_index, region))
            sent = low_back(first + zero_part)
            second = swin_layer(sent, second_params, True, rel_index, region)
            loss = jnp.sum(second * cot_part * keep_part[:, None, None])
            return (loss, first, second)
        losses, firsts, seconds = lax.map(jax.checkpoint(block), (inputs, zero_pad, cotangent, keep))
        return (jnp.sum(losses), (firsts, seconds))
    loss, back_fn, outputs = jax.vjp(total, inputs, zero_pad, params, has_aux=True)
    d_inputs, d_zero, d_params = back_fn(jnp.ones((), jnp.float32))
    firsts, seconds = outputs
    layer_out = jnp.stack([firsts, seconds]).reshape(2, IMAGES, TOK, D).astype(jnp.bfloat16)
    input_grad = jnp.stack([d_inputs, d_zero]).reshape(2, IMAGES, TOK, D).astype(jnp.bfloat16)
    return (layer_out, input_grad, d_params[0], d_params[1], d_params[2], d_params[3], d_params[4], d_params[5], d_params[6], d_params[7], d_params[5][:, 1])
```

```python
import functools

import jax
import jax.numpy as jnp
import numpy as np
from jax import lax
from jax.experimental import pallas as pl
from jax.experimental.pallas import tpu as pltpu
from jax.sharding import PartitionSpec as P

D = 512
FF = 2048
HEADS = 16
HEAD_DIM = 32
GRID = 14
WIN = 7
TOK = 196
WTOK = 49
NWIN = 4
TABLE = 169
MB = 2
PAIR = 112
ROWS = 2 * PAIR
LANES = 128
GROUP = LANES // HEAD_DIM

EPS = 1e-05
SCALE = HEAD_DIM ** (-0.5)
NEG = -1e30
HIGH = lax.Precision.HIGHEST
F32 = jnp.float32
BF16 = jnp.bfloat16


def order_matrix(layer):
    moved = (WIN // 2) if layer else 0
    place = np.zeros((ROWS, TOK), np.float32)
    for wi in range(2):
        for wj in range(2):
            for ti in range(WIN):
                for tj in range(WIN):
                    row = wi * PAIR + wj * WTOK + ti * WIN + tj
                    i = (wi * WIN + ti + moved) % GRID
                    j = (wj * WIN + tj + moved) % GRID
                    place[row, i * GRID + j] = 1.0
    return place


def dot(a, b):
    return lax.dot_general(a, b, (((1,), (0,)), ((), ())), preferred_element_type=F32)


def dot_nt(a, b):
    return lax.dot_general(a, b, (((1,), (1,)), ((), ())), preferred_element_type=F32)


def dot_tn(a, b):
    return lax.dot_general(a, b, (((0,), (0,)), ((), ())), preferred_element_type=F32)


def normalised(values):
    centred = values - jnp.mean(values, -1, keepdims=True)
    inverse = lax.rsqrt(jnp.mean(centred * centred, -1, keepdims=True) + EPS)
    return centred * inverse, inverse


def norm_back(upstream, gain, unit, inverse):
    d_unit = upstream * gain
    return inverse * (
        d_unit
        - jnp.mean(d_unit, -1, keepdims=True)
        - unit * jnp.mean(d_unit * unit, -1, keepdims=True)
    )


def head_masks():
    lane = lax.broadcasted_iota(jnp.int32, (PAIR, LANES), 1)
    return [
        jnp.where((lane >= j * HEAD_DIM) & (lane < (j + 1) * HEAD_DIM), 1.0, 0.0).astype(BF16)
        for j in range(GROUP)
    ]


def softmax(query, keys, bias):
    scores = dot_nt(query, keys) * SCALE + bias
    raised = jnp.exp(scores - jnp.max(scores, -1, keepdims=True))
    return raised / jnp.sum(raised, -1, keepdims=True)


def forward_kernel(
    place, place_t, x, qkv_w, proj_w, fc1_w, fc2_w, vec, hidden_bias, bias,
    y, windows, packed, mixed, middle, normed2, slope, active,
):
    source = dot(place[...], x[0])
    unit, _ = normalised(source)
    windows[0] = (unit * vec[0:1] + vec[2:3]).astype(BF16)
    win = windows[0]
    packed[0, :, :D] = (dot(win, qkv_w[:, :D]) + vec[3:4]).astype(BF16)
    packed[0, :, D : 2 * D] = dot(win, qkv_w[:, D : 2 * D]).astype(BF16)
    packed[0, :, 2 * D :] = (dot(win, qkv_w[:, 2 * D :]) + vec[4:5]).astype(BF16)
    masks = head_masks()
    for pair in range(2):
        rows = slice(pair * PAIR, (pair + 1) * PAIR)
        for group in range(HEADS // GROUP):
            at = group * LANES
            query = packed[0, rows, at : at + LANES]
            keys = packed[0, rows, D + at : D + at + LANES]
            values = packed[0, rows, 2 * D + at : 2 * D + at + LANES]
            total = None
            for j in range(GROUP):
                probs = softmax(query * masks[j], keys, bias[pair, group * GROUP + j])
                part = dot(probs.astype(BF16), values * masks[j])
                total = part if total is None else total + part
            mixed[0, rows, at : at + LANES] = total.astype(BF16)
    mid = source + dot(mixed[0], proj_w[...]) + vec[5:6]
    middle[0] = mid
    unit2, _ = normalised(mid)
    normed2[0] = (unit2 * vec[1:2] + vec[6:7]).astype(BF16)
    low = normed2[0]
    for c in range(FF // D):
        cols = slice(c * D, (c + 1) * D)
        hidden = dot(low, fc1_w[:, cols]) + hidden_bias[0:1, cols]
        half = 0.5 * (1.0 + lax.erf(hidden * 0.7071067811865476))
        active[0, :, cols] = (hidden * half).astype(BF16)
        bell = jnp.exp(-0.5 * hidden * hidden) * 0.3989422804014327
        slope[0, :, cols] = (half + hidden * bell).astype(BF16)
    out = mid + (dot(active[0], fc2_w[...]) + vec[7:8])
    y[0] = dot(place_t[...], out.astype(BF16)).astype(BF16)


def backward_kernel(
    place, place_t, x, up, qkv_w, proj_w, fc1_w, fc2_w, vec, bias, packed, middle, slope,
    d_x, up_rows, d_hidden, d_projected, d_packed, d_vec, d_hidden_bias, d_rel,
):
    @pl.when(pl.program_id(0) == 0)
    def _():
        d_vec[...] = jnp.zeros_like(d_vec)
        d_hidden_bias[...] = jnp.zeros_like(d_hidden_bias)
        d_rel[...] = jnp.zeros_like(d_rel)

    def add_row(row, values):
        d_vec[row : row + 1] += jnp.sum(values, 0, keepdims=True)

    upstream = dot(place[...], up[0])
    up_low = upstream.astype(BF16)
    up_rows[0] = up_low
    add_row(7, upstream)
    for c in range(FF // D):
        cols = slice(c * D, (c + 1) * D)
        d_active = dot_nt(up_low, fc2_w[cols])
        d_hid = (slope[0, :, cols].astype(F32) * d_active).astype(BF16)
        d_hidden[0, :, cols] = d_hid
        d_hidden_bias[0:1, cols] += jnp.sum(d_hid.astype(F32), 0, keepdims=True)
    d_normed2 = dot_nt(d_hidden[0], fc1_w[...])
    unit2, inverse2 = normalised(middle[0])
    add_row(1, d_normed2 * unit2)
    add_row(6, d_normed2)
    d_middle = upstream + norm_back(d_normed2, vec[1:2], unit2, inverse2)
    d_proj = d_middle.astype(BF16)
    d_projected[0] = d_proj
    add_row(5, d_proj.astype(F32))
    d_mixed = dot_nt(d_proj, proj_w[...]).astype(BF16)
    masks = head_masks()
    for pair in range(2):
        rows = slice(pair * PAIR, (pair + 1) * PAIR)
        for group in range(HEADS // GROUP):
            at = group * LANES
            query = packed[0, rows, at : at + LANES]
            keys = packed[0, rows, D + at : D + at + LANES]
            values = packed[0, rows, 2 * D + at : 2 * D + at + LANES]
            d_mix = d_mixed[rows, at : at + LANES]
            d_query = d_keys = d_values = None
            for j in range(GROUP):
                head = group * GROUP + j
                query_j = query * masks[j]
                d_mix_j = d_mix * masks[j]
                probs = softmax(query_j, keys, bias[pair, head])
                d_probs = dot_nt(d_mix_j, values)
                d_scores = probs * (d_probs - jnp.sum(probs * d_probs, -1, keepdims=True))
                d_low = d_scores.astype(BF16)
                d_rel[head] += d_low.astype(F32)
                one = dot(d_low, keys * masks[j])
                two = dot_tn(d_low, query_j)
                three = dot_tn(probs.astype(BF16), d_mix_j)
                d_query = one if j == 0 else d_query + one
                d_keys = two if j == 0 else d_keys + two
                d_values = three if j == 0 else d_values + three
            d_packed[0, rows, at : at + LANES] = (d_query * SCALE).astype(BF16)
            d_packed[0, rows, D + at : D + at + LANES] = (d_keys * SCALE).astype(BF16)
            d_packed[0, rows, 2 * D + at : 2 * D + at + LANES] = d_values.astype(BF16)
    add_row(3, d_packed[0, :, :D].astype(F32))
    add_row(4, d_packed[0, :, 2 * D :].astype(F32))
    d_windows = dot_nt(d_packed[0], qkv_w[...])
    unit, inverse = normalised(dot(place[...], x[0]))
    add_row(0, d_windows * unit)
    add_row(2, d_windows)
    d_source = d_middle + norm_back(d_windows, vec[0:1], unit, inverse)
    d_x[0] = dot(place_t[...], d_source.astype(BF16)).astype(BF16)


def whole(shape):
    return pl.BlockSpec(shape, lambda i: (0,) * len(shape))


def each(rows, cols):
    return pl.BlockSpec((1, rows, cols), lambda i: (i, 0, 0))


PARAMS = pltpu.CompilerParams(
    dimension_semantics=("arbitrary",), vmem_limit_bytes=58 * 1024 * 1024
)
WEIGHT_SPECS = [whole((D, 3 * D)), whole((D, D)), whole((D, FF)), whole((FF, D))]
BIAS_SHAPE = (2, HEADS, PAIR, PAIR)


def layer_forward(x, order, weights, vec, hidden_bias, bias):
    count = x.shape[0]
    saved = [(D, BF16), (3 * D, BF16), (D, BF16), (D, F32), (D, BF16), (FF, BF16), (FF, BF16)]
    return pl.pallas_call(
        forward_kernel,
        grid=(count,),
        in_specs=[whole((ROWS, TOK)), whole((TOK, ROWS)), each(TOK, D)]
        + WEIGHT_SPECS
        + [whole((8, D)), whole((1, FF)), whole(BIAS_SHAPE)],
        out_specs=[each(TOK, D)] + [each(ROWS, width) for width, _ in saved],
        out_shape=[jax.ShapeDtypeStruct((count, TOK, D), BF16)]
        + [jax.ShapeDtypeStruct((count, ROWS, width), kind) for width, kind in saved],
        compiler_params=PARAMS,
        cost_estimate=pl.CostEstimate(
            flops=count * 2_000_000_000, bytes_accessed=20_000_000, transcendentals=0
        ),
        name="layer_forward",
    )(*order, x, *weights, vec, hidden_bias, bias)


def layer_backward(x, up, order, weights, vec, bias, packed, middle, slope):
    count = x.shape[0]
    rows = [(D, BF16), (FF, BF16), (D, BF16), (3 * D, BF16)]
    sums = [(8, D), (8, FF), (HEADS, PAIR, PAIR)]
    return pl.pallas_call(
        backward_kernel,
        grid=(count,),
        in_specs=[whole((ROWS, TOK)), whole((TOK, ROWS)), each(TOK, D), each(TOK, D)]
        + WEIGHT_SPECS
        + [whole((8, D)), whole(BIAS_SHAPE), each(ROWS, 3 * D), each(ROWS, D), each(ROWS, FF)],
        out_specs=[each(TOK, D)]
        + [each(ROWS, width) for width, _ in rows]
        + [whole(shape) for shape in sums],
        out_shape=[jax.ShapeDtypeStruct((count, TOK, D), BF16)]
        + [jax.ShapeDtypeStruct((count, ROWS, width), kind) for width, kind in rows]
        + [jax.ShapeDtypeStruct(shape, F32) for shape in sums],
        compiler_params=PARAMS,
        cost_estimate=pl.CostEstimate(
            flops=count * 5_000_000_000, bytes_accessed=30_000_000, transcendentals=0
        ),
        name="layer_backward",
    )(*order, x, up, *weights, vec, bias, packed, middle, slope)


def swap(block):
    return lax.ppermute(block, "section", [(0, 1), (1, 0)])


def both_layers(piece):
    return lax.all_gather(piece, "section", axis=0, tiled=True)


def bias_blocks(onehot, table, differs):
    rel = jnp.dot(onehot, table, precision=HIGH).T.reshape(1, HEADS, WTOK, WTOK)
    if differs is None:
        blocks = jnp.broadcast_to(rel, (NWIN, HEADS, WTOK, WTOK))
    else:
        blocks = rel + jnp.where(differs, -100.0, 0.0)[:, None]
    blocks = blocks.reshape(2, 2, HEADS, WTOK, WTOK)
    last = PAIR - 2 * WTOK
    first = jnp.pad(
        blocks[:, 0], ((0, 0), (0, 0), (0, 0), (0, WTOK + last)), constant_values=NEG
    )
    second = jnp.pad(blocks[:, 1], ((0, 0), (0, 0), (0, 0), (WTOK, last)), constant_values=NEG)
    joined = jnp.concatenate([first, second], 2)
    return jnp.pad(joined, ((0, 0), (0, 0), (0, last), (0, 0)), constant_values=NEG)


def weight_sums(saved, grads, wide):
    windows, mixed, normed2, active = (v.reshape(-1, v.shape[-1]) for v in saved)
    up_rows, d_hidden, d_projected, d_packed = (v.reshape(-1, v.shape[-1]) for v in grads)
    g_fc2 = dot_tn(active, up_rows).astype(BF16)
    g_fc1 = dot_tn(normed2, d_hidden).astype(BF16)
    g_proj = dot_tn(mixed, d_projected).astype(BF16)
    g_qkv = dot_tn(windows, d_packed).astype(BF16)
    blocks = [g_fc2.reshape(wide, -1, D), g_proj.reshape(wide, -1, D)]
    blocks += [g_qkv[:, c * D : (c + 1) * D].reshape(wide, -1, D) for c in range(3)]
    blocks += [g_fc1[:, c * D : (c + 1) * D].reshape(wide, -1, D) for c in range(FF // D)]
    joined = jnp.concatenate(blocks, 1).reshape(-1, D)
    return lax.psum_scatter(
        joined, ("fsdp", "dp", "section"), scatter_dimension=0, tiled=True
    )


def body(
    images, out_grad, live, qkv_w, proj_w, fc1_w, fc2_w, gains, biases, hidden_bias, table,
    rel_index, region,
):
    section = lax.axis_index("section")
    wide = lax.axis_size("fsdp")
    count = images.shape[0] // MB
    mine = lax.dynamic_slice_in_dim(images, section * count, count, 0)
    cotangent = lax.dynamic_slice_in_dim(out_grad, section * count, count, 0)
    limit = lax.dynamic_slice_in_dim(live[0], section, 1, 0)
    keep = jnp.arange(count, dtype=jnp.int32) < limit
    cotangent = jnp.where(keep[:, None, None], cotangent, jnp.zeros((), BF16))

    gathered = [
        both_layers(lax.all_gather(w, "fsdp", axis=1, tiled=True))
        for w in (qkv_w, proj_w, fc1_w, fc2_w)
    ]
    joined = jnp.concatenate([gains, biases, hidden_bias.reshape(1, -1, gains.shape[-1])], 1)
    joined = both_layers(lax.all_gather(joined, "fsdp", axis=0, tiled=False))
    joined = joined.reshape(2, wide, -1, gains.shape[-1]).astype(F32)
    tables = both_layers(table)
    onehot = (rel_index.reshape(-1)[:, None] == jnp.arange(TABLE, dtype=jnp.int32)[None, :]).astype(
        F32
    )
    region_win = region.reshape(2, WIN, 2, WIN).transpose(0, 2, 1, 3).reshape(NWIN, WTOK)
    differs = region_win[:, :, None] != region_win[:, None, :]

    layers = []
    for layer in range(2):
        vec = joined[layer, :, :8].transpose(1, 0, 2).reshape(8, D)
        hidden = joined[layer, :, 8:].reshape(1, FF)
        bias = bias_blocks(onehot, tables[layer], differs if layer else None)
        place = order_matrix(layer)
        order = (jnp.asarray(place, BF16), jnp.asarray(place.T, BF16))
        layers.append((order, tuple(w[layer] for w in gathered), vec, hidden, bias))

    kept = []
    x = mine
    for order, weights, vec, hidden, bias in layers:
        y, *saved = layer_forward(x, order, weights, vec, hidden, bias)
        kept.append((x, saved))
        x = y
    outs = (kept[1][0], x)

    up = cotangent
    input_grads, pieces, smalls = [None, None], [None, None], [None, None]
    for layer in (1, 0):
        order, weights, vec, _, bias = layers[layer]
        source, (windows, packed, mixed, middle, normed2, slope, active) = kept[layer]
        up, *rows, d_vec, d_hidden_bias, d_rel = layer_backward(
            source, up, order, weights, vec, bias, packed, middle, slope
        )
        input_grads[layer] = up
        pieces[layer] = weight_sums((windows, mixed, normed2, active), rows, wide)
        d_rel = d_rel[:, :WTOK, :WTOK] + d_rel[:, WTOK : 2 * WTOK, WTOK : 2 * WTOK]
        d_table = jnp.einsum("pt,hp->th", onehot, d_rel.reshape(HEADS, -1), precision=HIGH)
        smalls[layer] = jnp.concatenate(
            [d_vec.reshape(-1), d_hidden_bias[0], d_table.reshape(-1)]
        )

    total = lax.psum(jnp.stack(smalls), ("section", "dp", "fsdp"))
    total = lax.dynamic_index_in_dim(total, section, 0, keepdims=False)
    part = lax.axis_index("fsdp")
    d_vec = total[: 8 * D].reshape(8, D)
    d_vec = lax.dynamic_slice_in_dim(d_vec, part * (D // wide), D // wide, 1)
    d_hidden_bias = lax.dynamic_slice_in_dim(
        total[8 * D : 8 * D + FF], part * (FF // wide), FF // wide, 0
    )
    d_table = total[8 * D + FF :].reshape(TABLE, HEADS)

    first_half = section == 0

    def exchange(first, second):
        own = jnp.where(first_half, first, second)
        other = swap(jnp.where(first_half, second, first))
        return jnp.concatenate(
            [jnp.where(first_half, own, other), jnp.where(first_half, other, own)], 0
        )

    layer_out = exchange(*outs)
    input_grad = exchange(*input_grads)
    own = exchange(*pieces)
    rows = lax.all_gather(own, "dp", axis=0, tiled=True).astype(F32)
    deep, thin = FF // wide, D // wide
    o_fc2, rows = rows[:deep], rows[deep:]
    o_proj, rows = rows[:thin], rows[thin:]
    o_qkv = jnp.concatenate([rows[c * thin : (c + 1) * thin] for c in range(3)], 1)
    rows = rows[3 * thin :]
    o_fc1 = jnp.concatenate([rows[c * thin : (c + 1) * thin] for c in range(FF // D)], 1)
    return (
        layer_out[None],
        input_grad[None],
        o_qkv[None],
        o_proj[None],
        o_fc1[None],
        o_fc2[None],
        d_vec[:2][None],
        d_vec[2:][None],
        d_hidden_bias[None],
        d_table[None],
        d_vec[3][None],
    )


def solution(mesh):
    return jax.shard_map(
        body,
        mesh=mesh,
        in_specs=(
            P(("dp", "fsdp"), None, None),
            P(("dp", "fsdp"), None, None),
            P(("dp", "fsdp"), None),
            P("section", "fsdp", None),
            P("section", "fsdp", None),
            P("section", "fsdp", None),
            P("section", "fsdp", None),
            P("section", None, "fsdp"),
            P("section", None, "fsdp"),
            P("section", "fsdp"),
            P("section", None, None),
            P(),
            P(),
        ),
        out_specs=(
            P("section", ("dp", "fsdp"), None, None),
            P("section", ("dp", "fsdp"), None, None),
            P("section", "fsdp", None),
            P("section", "fsdp", None),
            P("section", "fsdp", None),
            P("section", "fsdp", None),
            P("section", None, "fsdp"),
            P("section", None, "fsdp"),
            P("section", "fsdp"),
            P("section", None, None),
            P("section", "fsdp"),
        ),
        check_vma=False,
    )
```
